128 devices in a mesh: rows: 8 (over y_lo, x), blk: 16 (over y_hi, z, core).
Axes of the slice: x: 4, y: 4 (y_hi: 2, y_lo: 2; y = y_hi * 2 + y_lo), z: 4, core: 2. Of those that a mesh axis runs over, the one named last changes fastest.
Arguments:
- points: float32 [3, 262144], P(None, ('rows', 'blk')), may hold values from -6 to 6
- normals: float32 [3, 16384], P(None, ('rows', 'blk')), may hold values from -1 to 1
- weights: float32 [262144], P(('rows', 'blk')), may hold values from 0.25 to 1
- visible: int32 [512, 64], P(('rows', 'blk')), may hold values 0 or 1
- quad_mask: int32 [512, 64], P(('rows', 'blk')), may hold values from 1 to 65535
- owners: int32 [128, 256, 1], P(('rows', 'blk')), may hold values from 0 to 127; in each aligned block of 256 rows (0 to 255, 256 to 511, ..., all dimensions but the last counted through in order) at most 4 rows name the same one
Outputs:
- received: float32 [65536, 1024], P(('rows', 'blk'))
The draws below stay inside these ranges and needn't reach their ends.
Inputs may be any that keep to these rules, and one draw needn't show every extreme that they name: `owners`: among the 256 tiles of one device no owner is named more than 4 times, a bound that some block reaches.
All inputs are finite; a program needn't handle non-finite values. No bound on the sum of `visible` on one device may be relied on, other than what follows from the above.
Results may differ from the reference program's by a relative error of at most 0.0003.
Values sent between devices are 32-bit elements; how exact they have to be, the bound alone decides.
No kernel may reach another device: no remote copies, remote signals or barrier semaphores. Data moves between devices by JAX's collectives and lax.ppermute only.
A program may use at most 64 MiB of HBM per device.

```python
import math
import jax
import jax.numpy as jnp
import numpy as np
from jax import lax

Q = 16
TS = 32
P_DEV = 128
NP = 16384
NCOL = 2048
TILES_DEV = 256
CAP = 4
N_BLK = 16
DEVICES = 128


def with_ends(drawn, stream_key, smallest, largest):
    dims = drawn.shape
    index_at = [jax.random.randint(jax.random.fold_in(stream_key, axis), (), 0, dims[axis]) for axis in range(len(dims))]
    drawn = drawn.at[tuple(index_at)].set(smallest)
    longest = dims.index(max(dims))
    index_at[longest] = (index_at[longest] + 1) % dims[longest]
    return drawn.at[tuple(index_at)].set(largest)


def levels(own_key, extent, cuts, smallest, top_value):
    level, own = 1.0, jax.random.fold_in(own_key, 6)
    for axis_at, blocks in cuts:
        steps = jnp.exp(jax.random.uniform(jax.random.fold_in(own, axis_at), (blocks,), jnp.float32, smallest / len(cuts), top_value / len(cuts)))
        level = level * jnp.repeat(steps, extent[axis_at] // blocks).reshape([-1 if axis == axis_at else 1 for axis in range(len(extent))])
    return level


def deal_out(stream_key, own, number, rows, amount, top, limit, slope):
    sequence = jax.random.permutation(stream_key, amount)
    crowded, common = portions_of(amount, rows * top, limit, slope, True), portions_of(amount, rows * top, limit, slope, False)
    places = jnp.arange(amount)

    def named(sizes, offset_by):
        used = int((sizes > 0).sum())
        fixed = max(1, used // 4)
        shifted = fixed + (places - fixed + offset_by * (used - fixed)) % max(1, amount - fixed)
        return jnp.zeros((amount,), jnp.int32).at[sequence[jnp.where(places < fixed, places, shifted)]].set(jnp.asarray(sizes, jnp.int32))

    sizes = jnp.where(number % 4 == 0, named(crowded, number // 4), named(common, number - number // 4 - 1))
    mixed = jax.random.permutation(jax.random.fold_in(own, 3), amount)
    donor, taker = mixed[0:amount // 2 * 2:2], mixed[1:amount // 2 * 2:2]
    slack = jnp.minimum(sizes[donor] - 1, limit - sizes[taker]) // 2
    slack = jnp.where((donor == sequence[0]) | (taker == sequence[0]) | (sizes[taker] == 0), 0, jnp.maximum(slack, 0))
    shifted = jax.random.randint(jax.random.fold_in(own, 4), (amount // 2,), 0, 1 << 20) % (slack + 1)
    sizes = sizes.at[donor].add(-shifted).at[taker].add(shifted)
    members = jnp.searchsorted(jnp.cumsum(sizes), jnp.arange(rows * top), side="right").astype(jnp.int32)
    listing = members.reshape(top, rows).T
    listing = listing[jax.random.permutation(jax.random.fold_in(own, 1), rows)]
    offset_by = jax.random.randint(jax.random.fold_in(own, 2), (rows, 1), 0, top)
    return jnp.take_along_axis(listing, (jnp.arange(top)[None, :] + offset_by) % top, axis=1)


def portions_of(count, total, most, slope, full):
    weights = [(1 << 20) // math.isqrt(grade ** slope) + 1 for grade in range(1, count + 1)]
    largest = most if full else min(most, max(-(-total // count), total * weights[0] // sum(weights)))
    least = 1 if total - largest >= count - 1 else 0
    given, rest = [largest] + [least] * (count - 1), total - largest - least * (count - 1)
    while rest > 0:
        free = [i for i in range(1, count) if given[i] < largest] or [i for i in range(1, count) if given[i] < most]
        pool, left = sum([weights[i] for i in free]), rest
        for i in free:
            more = min(most - given[i], max(1, left * weights[i] // pool), rest)
            given[i] = given[i] + more
            rest = rest - more
    return np.array(given)


def bell_draw(rng, dims, deviation, reach, shards=(), kind=jnp.bfloat16):
    entries = jax.random.normal(rng, dims, jnp.float32) * deviation
    if len(shards) > 0:
        entries = levels(rng, dims, shards, -0.22, 0.18) * entries
    return jnp.clip(entries, min=-reach, max=reach).astype(kind)


def setup_inputs(seed: int = 0) -> dict:
    arg_keys = jax.random.split(jax.random.key(seed), 7)
    points = bell_draw(arg_keys[0], (3, NP * Q), 1.0, 6.0, ((1, 128),), jnp.float32)
    normals = jnp.clip(jax.random.uniform(arg_keys[1], (3, NP), jnp.float32, -1.0, 1.0) * levels(arg_keys[1], (3, NP), ((1, 128),), -0.4, 0.0), -1.0, 1.0)
    weights = jnp.clip(jnp.exp(math.log(1.0) - 1.3862944 * jax.random.uniform(arg_keys[2], (NP * Q,), jnp.float32) ** levels(arg_keys[2], (NP * Q,), ((0, 128),), -0.2, 0.2)), 0.25, 1.0)
    visible = with_ends((jax.random.randint(arg_keys[3], (NP // TS, NCOL // TS), 0, 4) < 3).astype(jnp.int32), jax.random.fold_in(arg_keys[3], 1), 0, 1)
    quad_mask = with_ends(jax.random.randint(arg_keys[4], (NP // TS, NCOL // TS), 1, 65536), jax.random.fold_in(arg_keys[4], 1), 1, 65535).astype(jnp.int32)
    owners_keys = jax.random.split(jax.random.fold_in(arg_keys[5], 1), DEVICES * TILES_DEV // TILES_DEV)
    owners_turns = jax.random.permutation(jax.random.fold_in(arg_keys[5], 3), DEVICES * TILES_DEV // TILES_DEV)
    owners = jax.vmap(lambda own, number: deal_out(jax.random.fold_in(arg_keys[5], 2), own, number, TILES_DEV, DEVICES, 1, CAP, 2))(owners_keys, owners_turns).reshape((DEVICES, TILES_DEV, 1))
    return dict(points=points, normals=normals, weights=weights, visible=visible, quad_mask=quad_mask, owners=owners)


softening = 0.05


def tile_bits(quad_mask):
    shifts = jnp.arange(Q, dtype=jnp.int32)
    return ((quad_mask[..., None] >> shifts) & 1).astype(jnp.float32)


def row_block(row_points, row_normals, row_weights, col_points, col_normals, col_weights, bits, seen):
    rows = row_normals.shape[1]
    patches = col_normals.shape[1]
    row_vecs = jnp.repeat(row_normals, Q, axis=1)
    col_vecs = jnp.repeat(col_normals, Q, axis=1)
    delta_x = col_points[0][None, :] - row_points[0][:, None]
    delta_y = col_points[1][None, :] - row_points[1][:, None]
    delta_z = col_points[2][None, :] - row_points[2][:, None]
    distance = delta_x * delta_x + delta_y * delta_y + delta_z * delta_z + softening
    cos_row = row_vecs[0][:, None] * delta_x + row_vecs[1][:, None] * delta_y + row_vecs[2][:, None] * delta_z
    cos_col = -(col_vecs[0][None, :] * delta_x + col_vecs[1][None, :] * delta_y + col_vecs[2][None, :] * delta_z)
    kernel = jnp.maximum(cos_row, 0.0) * jnp.maximum(cos_col, 0.0) / (math.pi * distance * distance)
    kernel = kernel * col_weights[None, :]
    summed = jnp.sum(kernel.reshape(rows * Q, patches, Q), axis=2).reshape(rows, Q, patches)
    quad_weights = row_weights.reshape(rows, Q)
    active = jnp.repeat(jnp.repeat(bits.transpose(0, 2, 1), TS, axis=0), TS, axis=2)
    seen_full = jnp.repeat(jnp.repeat(seen, TS, axis=0), TS, axis=1)
    folded = jnp.sum(summed * quad_weights[:, :, None] * active, axis=1)
    area = jnp.sum(quad_weights, axis=1)
    return folded / area[:, None] * seen_full


def to_tiles(factors):
    height, width = factors.shape
    blocks = factors.reshape(height // TS, TS, width // TS, TS).transpose(0, 2, 1, 3)
    return blocks.reshape(-1, TS * TS)


def owner_slots(targets, tiles, owner_count, capacity):
    same_owner = targets[:, None] == targets[None, :]
    order = jnp.arange(targets.shape[0], dtype=jnp.int32)
    earlier = order[:, None] > order[None, :]
    rank = jnp.sum((same_owner & earlier).astype(jnp.int32), axis=1)
    slot = targets * capacity + rank
    empty = jnp.zeros((owner_count * capacity, tiles.shape[1]), tiles.dtype)
    return empty.at[slot].set(tiles)


def reference(points, normals, weights, visible, quad_mask, owners):
    region = N_BLK * P_DEV
    span = P_DEV // TS

    def device_rows(device):
        group = device // N_BLK
        row_points = lax.dynamic_slice_in_dim(points, device * (P_DEV * Q), P_DEV * Q, 1)
        row_normals = lax.dynamic_slice_in_dim(normals, device * P_DEV, P_DEV, 1)
        row_weights = lax.dynamic_slice_in_dim(weights, device * (P_DEV * Q), P_DEV * Q, 0)
        seen = lax.dynamic_slice_in_dim(visible, device * span, span, 0).astype(jnp.float32)
        bits = tile_bits(lax.dynamic_slice_in_dim(quad_mask, device * span, span, 0))
        blocks = []
        for source in range(N_BLK):
            start = group * region + source * P_DEV
            col_points = lax.dynamic_slice_in_dim(points, start * Q, P_DEV * Q, 1)
            col_normals = lax.dynamic_slice_in_dim(normals, start, P_DEV, 1)
            col_weights = lax.dynamic_slice_in_dim(weights, start * Q, P_DEV * Q, 0)
            block_bits = bits[:, source * span:(source + 1) * span]
            block_seen = seen[:, source * span:(source + 1) * span]
            blocks.append(row_block(row_points, row_normals, row_weights, col_points, col_normals, col_weights, block_bits, block_seen))
        factors = jnp.concatenate(blocks, axis=1)
        targets = lax.dynamic_index_in_dim(owners, device, 0, keepdims=False)[:, 0]
        return owner_slots(targets, to_tiles(factors), DEVICES, CAP)

    sends = lax.map(device_rows, jnp.arange(DEVICES, dtype=jnp.int32))
    return sends.reshape(DEVICES, DEVICES, CAP, TS * TS).transpose(1, 0, 2, 3).reshape(-1, TS * TS)
```

```python
import functools
import math

import jax
import jax.numpy as jnp
from jax import lax
from jax.experimental import pallas as pl
from jax.experimental.pallas import tpu as pltpu
from jax.sharding import PartitionSpec as P

Q = 16
TS = 32
GROUP = 4
softening = 0.05
BF = jnp.bfloat16
F32 = jnp.float32


def three_parts(x):
    high = x.astype(BF)
    rest = x - high.astype(F32)
    middle = rest.astype(BF)
    low = (rest - middle.astype(F32)).astype(BF)
    return high, middle, low


def features_kernel(cols_ref, norm_ref, out_ref):
    row = lax.broadcasted_iota(jnp.int32, (8, TS * Q), 0)
    for tile in range(cols_ref.shape[1]):
        cols = cols_ref[0, tile]
        x, y, z, w = (cols[f : f + 1] for f in range(4))
        normal = norm_ref[0, tile]
        nx, ny, nz = (jnp.concatenate([normal[f : f + 1]] * 4, axis=1) for f in range(3))
        square = x * x + y * y + z * z
        depth = nx * x + ny * y + nz * z
        scale = w * (1.0 / math.pi)
        pick = lambda *rows: functools.reduce(
            lambda acc, at: jnp.where(row == at, rows[at], acc), range(len(rows)), jnp.zeros((8, TS * Q), F32)
        )
        ours = pick(x, y, z, square, jnp.ones_like(x))
        half = scale * -0.5
        theirs = pick(nx * half, ny * half, nz * half, -depth * scale)
        both = jnp.concatenate([ours, theirs], axis=1)
        high = both.astype(BF).astype(F32)
        rest = both - high
        middle = rest.astype(BF).astype(F32)
        low = rest - middle
        out_ref[tile] = jnp.concatenate([high, high, high, middle, middle, low], axis=0).astype(BF)


def features(cols, normals):
    sources, span = cols.shape[:2]
    width = TS * Q
    return pl.pallas_call(
        features_kernel,
        grid=(sources,),
        in_specs=[
            pl.BlockSpec((1, span, 4, width), lambda s: (s, 0, 0, 0)),
            pl.BlockSpec((1, span, 3, 128), lambda s: (s, 0, 0, 0)),
        ],
        out_specs=pl.BlockSpec((span, 48, 2 * width), lambda s: (s, 0, 0)),
        out_shape=jax.ShapeDtypeStruct((sources * span, 48, 2 * width), BF),
        compiler_params=pltpu.CompilerParams(vmem_limit_bytes=40 * 2**20),
    )(cols, normals)


def tiles_kernel(total_ref, groups_ref, units_ref, lhs_ref, rhs_ref, out_ref):
    out_ref[...] = jnp.zeros_like(out_ref)
    lane = lax.broadcasted_iota(jnp.int32, (8, 128), 1)
    odd = (lane // TS) % 2 == 1
    upper = lane // (2 * TS) == 1
    width = TS * Q
    last = groups_ref.shape[0] - 1

    def one_group(_, carry):
        tile, at = carry
        codes = [units_ref[tile * 64 + at * GROUP + g] for g in range(GROUP)]
        rows = [code % 128 for code in codes]
        gap = jnp.concatenate([lhs_ref[r, :TS] for r in rows], axis=0)
        facing = jnp.concatenate([lhs_ref[r, TS:] for r in rows], axis=0)
        sums = [None] * (GROUP * 4)
        for part in range(width // 256):
            ours = rhs_ref[tile, :, part * 256 : (part + 1) * 256]
            theirs = rhs_ref[tile, :, width + part * 256 : width + (part + 1) * 256]
            spread = jnp.dot(gap, ours, preferred_element_type=F32)
            cos_row = jnp.dot(facing, ours, preferred_element_type=F32)
            cos_col = jnp.dot(gap, theirs, preferred_element_type=F32)
            value = (
                jnp.maximum(cos_row, 0.0)
                * jnp.maximum(cos_col, 0.0)
                * pl.reciprocal(spread * spread, approx=True)
            )
            for v in range(GROUP * 4):
                piece = value[v * 8 : v * 8 + 8]
                piece = piece[:, :128] + piece[:, 128:]
                sums[v] = piece if sums[v] is None else sums[v] + piece
        for g in range(GROUP):
            a0, a1, a2, a3 = sums[g * 4 : g * 4 + 4]
            low = jnp.where(odd, a1, a0) + pltpu.roll(jnp.where(odd, a0, a1), TS, 1)
            high = jnp.where(odd, a3, a2) + pltpu.roll(jnp.where(odd, a2, a3), TS, 1)
            mixed = jnp.where(upper, high, low) + pltpu.roll(jnp.where(upper, low, high), 2 * TS, 1)
            slot = codes[g] // 128
            out_ref[slot] = out_ref[slot] + mixed
        done = at + 1 >= groups_ref[tile]
        return (jnp.where(done, jnp.minimum(tile + 1, last), tile), jnp.where(done, 0, at + 1))

    lax.fori_loop(0, total_ref[0], one_group, (jnp.int32(0), jnp.int32(0)))


def assemble(total, groups, units, lhs, rhs, slots):
    smem = pl.BlockSpec(memory_space=pltpu.SMEM)
    vmem = pl.BlockSpec(memory_space=pltpu.VMEM)
    return pl.pallas_call(
        tiles_kernel,
        in_specs=[smem, smem, smem, vmem, vmem],
        out_specs=vmem,
        out_shape=jax.ShapeDtypeStruct((slots, 8, 128), F32),
        compiler_params=pltpu.CompilerParams(vmem_limit_bytes=56 * 2**20),
    )(total, groups, units, lhs, rhs)


def rounded(x):
    return lax.reduce_precision(x, 8, 7)


def row_features(points, normals, weights):
    span = normals.shape[1] // TS
    area = jnp.sum(weights.reshape(-1, Q), axis=1, keepdims=True)
    scale = (area / weights.reshape(-1, Q)).reshape(-1)
    x, y, z = points
    nx, ny, nz = jnp.repeat(normals, Q, axis=1)
    square = x * x + y * y + z * z + softening
    depth = nx * x + ny * y + nz * z
    zero = jnp.zeros_like(x)
    gap = [-2.0 * x * scale, -2.0 * y * scale, -2.0 * z * scale, scale, square * scale, zero, zero, zero]
    facing = [nx, ny, nz, zero, -depth, zero, zero, zero]
    rows = jnp.stack([jnp.stack(gap), jnp.stack(facing)])
    rows = rows.reshape(2, 8, span, 8, 4, Q).transpose(2, 5, 0, 4, 3, 1)
    rows = rows.reshape(span * Q, 2 * TS, 8)
    pad = jnp.zeros((1, 2 * TS, 8), F32).at[0, :TS, 4].set(1.0)
    rows = jnp.concatenate([rows, pad])
    high = rounded(rows)
    middle = rounded(rows - high)
    low = rounded(rows - high - middle)
    return jnp.concatenate([high, middle, low, high, middle, high], axis=2).astype(BF)


def work_list(visible, quad_mask, targets, capacity):
    span, columns = visible.shape
    order = jnp.arange(targets.shape[0], dtype=jnp.int32)
    same = targets[:, None] == targets[None, :]
    rank = jnp.sum((same & (order[:, None] > order[None, :])).astype(jnp.int32), axis=1)
    slot = (targets * capacity + rank).reshape(span, columns)
    shifts = jnp.arange(Q, dtype=jnp.int32)
    used = ((quad_mask[:, None, :] >> shifts[None, :, None]) & 1) * visible[:, None, :]
    pair = jnp.arange(span * Q, dtype=jnp.int32)
    code = (slot[:, None, :] * 128 + pair.reshape(span, Q)[:, :, None]).reshape(span * Q, columns)
    used = used.reshape(span * Q, columns)
    place = jnp.sum(jnp.where(pair[:, None] > pair[None, :], 1, 0)[:, :, None] * used[None], axis=1)
    count = jnp.sum(used, axis=0)
    idle = span * Q
    hit = (place[:, None, :] == pair[None, :, None]) & (used[:, None, :] > 0)
    units = jnp.sum(jnp.where(hit, code[:, None, :] - idle, 0), axis=0) + idle
    groups = jnp.maximum((count + GROUP - 1) // GROUP, 1)
    return jnp.sum(groups)[None], groups, units.T.reshape(-1)


def on_device(points, normals, weights, visible, quad_mask, owners):
    devices = lax.axis_size("rows") * lax.axis_size("blk")
    sources = lax.axis_size("blk")
    span = normals.shape[1] // TS
    capacity = max(2, 2 * owners.shape[1] // devices)
    flat = jnp.concatenate([points, weights[None]])
    cols = flat.reshape(4, span, TS, Q).transpose(1, 0, 3, 2).reshape(-1, 128)
    tiled = jnp.tile(normals.reshape(3, span, 1, TS).transpose(1, 0, 2, 3), (1, 1, 4, 1)).reshape(-1, 128)
    packed = jnp.concatenate([cols, tiled, jnp.zeros((-(cols.shape[0] + tiled.shape[0]) % 8, 128), F32)])
    spread = jnp.broadcast_to(packed[None], (sources,) + packed.shape)
    gathered = lax.all_to_all(spread, "blk", split_axis=0, concat_axis=0, tiled=True)
    all_cols = gathered[:, : cols.shape[0]].reshape(sources, span, 4, TS * Q)
    all_normals = gathered[:, cols.shape[0] : cols.shape[0] + tiled.shape[0]].reshape(sources, span, 3, 128)
    rhs = features(all_cols, all_normals)
    lhs = row_features(points, normals, weights)
    total, groups, units = work_list(visible, quad_mask, owners[0, :, 0], capacity)
    out = assemble(total, groups, units, lhs, rhs, devices * capacity)
    arrived = lax.all_to_all(
        out.reshape(devices, capacity * 8, 128), ("rows", "blk"), split_axis=0, concat_axis=0, tiled=True
    )
    return arrived.reshape(devices * capacity, TS * TS)


def solution(mesh):
    placed = (
        P(None, ("rows", "blk")),
        P(None, ("rows", "blk")),
        P(("rows", "blk")),
        P(("rows", "blk"), None),
        P(("rows", "blk"), None),
        P(("rows", "blk"), None, None),
    )
    return jax.shard_map(
        on_device, mesh=mesh, in_specs=placed, out_specs=P(("rows", "blk"), None), check_vma=False
    )
```

```python
import functools
import math

import jax
import jax.numpy as jnp
from jax import lax
from jax.experimental import pallas as pl
from jax.experimental.pallas import tpu as pltpu
from jax.sharding import PartitionSpec as P

Q = 16
TS = 32
GROUP = 4
FOLD = 16
softening = 0.05
BF = jnp.bfloat16
F32 = jnp.float32


def split(x):
    high = x.astype(BF).astype(F32)
    rest = x - high
    middle = rest.astype(BF).astype(F32)
    return high, middle, rest - middle


def by_rows(shape, values, axis=0):
    at = lax.broadcasted_iota(jnp.int32, shape, axis)
    return functools.reduce(
        lambda acc, k: jnp.where(at == k, values[k], acc), range(len(values)), jnp.zeros(shape, F32)
    )


def exact_dot(parts, selector, contract=((1,), (0,))):
    dots = [lax.dot_general(part.astype(BF), selector, (contract, ((), ())), preferred_element_type=F32) for part in parts]
    return dots[0] + dots[1] + dots[2]


def rows_kernel(points_ref, weights_ref, normals_ref, gap_ref, depth_ref, face_ref):
    width = TS * Q
    span = normals_ref.shape[1] // TS
    iota = lambda shape, axis: lax.broadcasted_iota(jnp.int32, shape, axis)
    as_ones = lambda hit: jnp.where(hit, 1.0, 0.0).astype(BF)
    row = iota((width, 1), 0)
    order = as_ones(iota((width, width), 1) == (row % 8) * 64 + (row // 8 % 4) * Q + row // TS)
    same = as_ones(iota((width, width), 1) // Q == iota((width, width), 0) // Q)
    widen = as_ones(iota((TS, width), 1) // Q == iota((TS, width), 0))
    small = iota((TS, 1), 0)
    shuffle = as_ones(iota((TS, TS), 1) == (small % 8) * 4 + small // 8)
    across = ((1,), (1,))
    for top in range(span):
        at = slice(top * width, (top + 1) * width)
        x, y, z = (points_ref[k : k + 1, at] for k in range(3))
        weight = weights_ref[:, at]
        normal = normals_ref[:, top * TS : (top + 1) * TS]
        normal = jnp.concatenate([normal, jnp.zeros((5, TS), F32)], axis=0)
        high, middle, low = split(normal)
        face = jnp.concatenate([high, middle, low, high, middle, high], axis=0).astype(BF)
        face = lax.dot_general(shuffle, face, (across, ((), ())), preferred_element_type=F32)
        face_ref[top * TS : (top + 1) * TS] = face.astype(BF)
        wide = exact_dot((high, middle, low), widen)
        depth = wide[0:1] * x + wide[1:2] * y + wide[2:3] * z
        area = exact_dot(split(jnp.broadcast_to(weight, (8, width))), same)[0:1]
        scale = area / weight
        square = x * x + y * y + z * z + softening
        gap = by_rows((8, width), [-2.0 * x * scale, -2.0 * y * scale, -2.0 * z * scale, scale, square * scale])
        high, middle, low = split(gap)
        gap = jnp.concatenate([high, middle, low, high, middle, high], axis=0).astype(BF)
        gap = lax.dot_general(order, gap, (across, ((), ())), preferred_element_type=F32)
        gap_ref[top * Q : (top + 1) * Q] = gap.astype(BF).reshape(Q, TS, 48)
        parts = [jnp.broadcast_to(part, (128, width)).astype(BF) for part in split(depth)]
        deep = [lax.dot_general(order, part, (across, ((), ())), preferred_element_type=F32) for part in parts]
        depth_ref[top * Q : (top + 1) * Q] = (deep[0] + deep[1] + deep[2]).reshape(Q, TS, 128)
    gap_ref[span * Q] = jnp.where(iota((TS, 48), 1) == 4, 1.0, 0.0).astype(BF)
    depth_ref[span * Q] = jnp.zeros((TS, 128), F32)


def row_features(points, weights, normals):
    vmem = pl.BlockSpec(memory_space=pltpu.VMEM)
    pairs = normals.shape[1] // TS * Q + 1
    return pl.pallas_call(
        rows_kernel,
        in_specs=[vmem] * 3,
        out_specs=[vmem] * 3,
        out_shape=[
            jax.ShapeDtypeStruct((pairs, TS, 48), BF),
            jax.ShapeDtypeStruct((pairs, TS, 128), F32),
            jax.ShapeDtypeStruct((normals.shape[1], 48), BF),
        ],
        compiler_params=pltpu.CompilerParams(vmem_limit_bytes=40 * 2**20),
    )(points, weights, normals)


def column_features(packed_ref, rhs_ref, source):
    width = TS * Q
    span = rhs_ref.shape[0] // packed_ref.shape[0]
    for tile in range(span):
        base = span * Q + tile * 3
        nx, ny, nz = (packed_ref[source, base + k : base + k + 1] for k in range(3))
        for lanes in range(width // 128):
            at = tile * Q + lanes * 4
            x, y, z, w = (packed_ref[source, at + k : at + k + 1] for k in range(4))
            square = x * x + y * y + z * z
            depth = nx * x + ny * y + nz * z
            scale = w * (1.0 / math.pi)
            half = scale * -0.5
            ours = by_rows((8, 128), [x, y, z, square, jnp.ones_like(x)])
            theirs = by_rows((8, 128), [nx * half, ny * half, nz * half, -depth * scale])
            for block, start in ((ours, lanes * 128), (theirs, width + lanes * 128)):
                high, middle, low = split(block)
                rhs_ref[source * span + tile, :, start : start + 128] = jnp.concatenate(
                    [high, high, high, middle, middle, low], axis=0
                ).astype(BF)


def tiles_kernel(total_ref, groups_ref, units_ref, slot_ref, lhs_ref, depth_ref, face_ref, packed_ref, out_ref, acc, near, rhs_ref):
    out_ref[...] = jnp.zeros_like(out_ref)
    acc[...] = jnp.zeros_like(acc)
    width = TS * Q
    last = rhs_ref.shape[0] - 1

    def codes_of(place):
        tile, at = place
        return [units_ref[tile * 64 + at * GROUP + g] for g in range(GROUP)]

    def following(place):
        tile, at = place
        done = at + 1 >= groups_ref[tile]
        return (jnp.where(done, tile + 1, tile), jnp.where(done, 0, at + 1))

    def work_on(place):
        codes = codes_of(place)
        rows = [code % 128 for code in codes]
        tile = jnp.minimum(place[0], last)
        gap = jnp.concatenate([lhs_ref[r] for r in rows], axis=0)
        tops = [pl.ds(pl.multiple_of(jnp.minimum(r // Q, 3) * TS, TS), TS) for r in rows]
        total = [None] * GROUP
        for part in range(width // 256):
            at = slice(part * 256, (part + 1) * 256)
            ours = rhs_ref[tile, :, at]
            theirs = rhs_ref[tile, :, width + part * 256 : width + (part + 1) * 256]
            spread = jnp.dot(gap, ours, preferred_element_type=F32)
            cos_col = jnp.dot(gap, theirs, preferred_element_type=F32)
            value = jnp.maximum(cos_col, 0.0) * pl.reciprocal(spread * spread, approx=True)
            for g in range(GROUP):
                depth = depth_ref[rows[g]]
                for half in range(2):
                    lanes = slice(part * 256 + half * 128, part * 256 + (half + 1) * 128)
                    piece = jnp.maximum(near[tile, tops[g], lanes] - depth, 0.0) * value[g * TS : (g + 1) * TS, half * 128 : (half + 1) * 128]
                    total[g] = piece if total[g] is None else total[g] + piece
        return codes, total

    def some_groups(_, place):
        done = []
        for _ in range(8):
            done.append(work_on(place))
            place = following(place)
        for codes, total in done:
            for g in range(GROUP):
                tile = codes[g] // 128
                acc[tile] = acc[tile] + total[g]
        return place

    def gather(source, _):
        column_features(packed_ref, rhs_ref, source)
        return 0

    lax.fori_loop(0, packed_ref.shape[0], gather, 0)

    def faces(step, _):
        for k in range(2):
            near[step * 2 + k] = jnp.dot(face_ref[...], rhs_ref[step * 2 + k, :, :width], preferred_element_type=F32)
        return 0

    lax.fori_loop(0, rhs_ref.shape[0] // 2, faces, 0)
    lax.fori_loop(0, (total_ref[0] + 8 - 1) // 8, some_groups, (jnp.int32(0), jnp.int32(0)))

    lane = lax.broadcasted_iota(jnp.int32, (8, 128), 1)
    second = (lane // TS) % 2 == 1
    upper = lane // (2 * TS) == 1

    def fold(step, _):
        for k in range(FOLD):
            tile = step * FOLD + k
            a0, a1, a2, a3 = [acc[tile, v * 8 : v * 8 + 8] for v in range(4)]
            low = jnp.where(second, a1, a0) + pltpu.roll(jnp.where(second, a0, a1), TS, 1)
            high = jnp.where(second, a3, a2) + pltpu.roll(jnp.where(second, a2, a3), TS, 1)
            mixed = jnp.where(upper, high, low) + pltpu.roll(jnp.where(upper, low, high), 2 * TS, 1)
            out_ref[slot_ref[tile]] = mixed
        return 0

    lax.fori_loop(0, acc.shape[0] // FOLD, fold, 0)


def assemble(total, groups, units, slot, lhs, depth, face, packed, slots):
    smem = pl.BlockSpec(memory_space=pltpu.SMEM)
    vmem = pl.BlockSpec(memory_space=pltpu.VMEM)
    columns = units.shape[0] // 64 - 1
    return pl.pallas_call(
        tiles_kernel,
        in_specs=[smem] * 4 + [vmem] * 4,
        out_specs=vmem,
        out_shape=jax.ShapeDtypeStruct((slots, 8, 128), F32),
        scratch_shapes=[
            pltpu.VMEM((slot.shape[0], TS, 128), F32),
            pltpu.VMEM((columns, face.shape[0], TS * Q), F32),
            pltpu.VMEM((columns, 48, 2 * TS * Q), BF),
        ],
        compiler_params=pltpu.CompilerParams(vmem_limit_bytes=56 * 2**20),
    )(total, groups, units, slot, lhs, depth, face, packed)


def work_list(visible, quad_mask, targets, capacity):
    span, columns = visible.shape
    order = jnp.arange(targets.shape[0], dtype=jnp.int32)
    same = targets[:, None] == targets[None, :]
    rank = jnp.sum((same & (order[:, None] > order[None, :])).astype(jnp.int32), axis=1)
    slot = targets * capacity + rank
    shifts = jnp.arange(Q, dtype=jnp.int32)
    used = ((quad_mask[:, None, :] >> shifts[None, :, None]) & 1) * visible[:, None, :]
    pair = jnp.arange(span * Q, dtype=jnp.int32)
    name = order.reshape(span, columns)
    code = (name[:, None, :] * 128 + pair.reshape(span, Q)[:, :, None]).reshape(span * Q, columns)
    used = used.reshape(span * Q, columns)
    place = jnp.sum(jnp.where(pair[:, None] > pair[None, :], 1, 0)[:, :, None] * used[None], axis=1)
    count = jnp.sum(used, axis=0)
    idle = span * Q
    hit = (place[:, None, :] == pair[None, :, None]) & (used[:, None, :] > 0)
    units = jnp.sum(jnp.where(hit, code[:, None, :] - idle, 0), axis=0) + idle
    groups = jnp.maximum((count + GROUP - 1) // GROUP, 1)
    spare = jnp.full((units.shape[0],), idle, jnp.int32)
    groups = jnp.concatenate([groups, jnp.full((1,), Q, jnp.int32)])
    return jnp.sum(groups[:-1])[None], groups, jnp.concatenate([units.T.reshape(-1), spare]), slot


def pack_columns(points, weights, normals):
    span = normals.shape[1] // TS
    flat = jnp.concatenate([points, weights[None]])
    cols = flat.reshape(4, span, TS, 4, 4).transpose(1, 3, 0, 4, 2).reshape(-1, 128)
    tiled = jnp.tile(normals.reshape(3, span, 1, TS).transpose(1, 0, 2, 3), (1, 1, 4, 1)).reshape(-1, 128)
    return jnp.concatenate([cols, tiled, jnp.zeros((-(cols.shape[0] + tiled.shape[0]) % 8, 128), F32)])


def on_device(points, normals, weights, visible, quad_mask, owners):
    devices = lax.axis_size("rows") * lax.axis_size("blk")
    sources = lax.axis_size("blk")
    capacity = max(2, 2 * owners.shape[1] // devices)
    packed = pack_columns(points, weights, normals)
    spread = jnp.broadcast_to(packed[None], (sources,) + packed.shape)
    gathered = lax.all_to_all(spread, "blk", split_axis=0, concat_axis=0, tiled=True)
    lhs, depth, face = row_features(points, weights[None], normals)
    total, groups, units, slot = work_list(visible, quad_mask, owners[0, :, 0], capacity)
    out = assemble(total, groups, units, slot, lhs, depth, face, gathered, devices * capacity)
    arrived = lax.all_to_all(
        out.reshape(devices, capacity * 8, 128), ("rows", "blk"), split_axis=0, concat_axis=0, tiled=True
    )
    return arrived.reshape(devices * capacity, TS * TS)


def solution(mesh):
    placed = (
        P(None, ("rows", "blk")),
        P(None, ("rows", "blk")),
        P(("rows", "blk")),
        P(("rows", "blk"), None),
        P(("rows", "blk"), None),
        P(("rows", "blk"), None, None),
    )
    return jax.shard_map(
        on_device, mesh=mesh, in_specs=placed, out_specs=P(("rows", "blk"), None), check_vma=False
    )
```

```python
import functools
import math

import jax
import jax.numpy as jnp
from jax import lax
from jax.experimental import pallas as pl
from jax.experimental.pallas import tpu as pltpu
from jax.sharding import PartitionSpec as P

Q = 16
TS = 32
GROUP = 4
FOLD = 32
DEEP = 32
softening = 0.05
BF = jnp.bfloat16
F32 = jnp.float32


def split(x):
    high = x.astype(BF).astype(F32)
    rest = x - high
    middle = rest.astype(BF).astype(F32)
    return high, middle, rest - middle


def by_rows(shape, values, axis=0):
    at = lax.broadcasted_iota(jnp.int32, shape, axis)
    return functools.reduce(
        lambda acc, k: jnp.where(at == k, values[k], acc), range(len(values)), jnp.zeros(shape, F32)
    )


def exact_dot(parts, selector, contract=((1,), (0,))):
    dots = [lax.dot_general(part.astype(BF), selector, (contract, ((), ())), preferred_element_type=F32) for part in parts]
    return dots[0] + dots[1] + dots[2]


def list_work(visible_ref, mask_ref, across_ref, down_ref, capacity, total_ref, groups_ref, units_ref, slot_ref):
    span, columns = visible_ref.shape
    tiles = across_ref.shape[1]
    pairs = span * Q
    iota = lambda shape, axis: lax.broadcasted_iota(jnp.int32, shape, axis)
    earlier = (across_ref[...] == down_ref[...]) & (iota((tiles, tiles), 0) < iota((tiles, tiles), 1))
    rank = jnp.sum(jnp.where(earlier, 1, 0), axis=0, keepdims=True)
    slot_ref[...] = across_ref[...] * capacity + rank
    point = iota((Q, columns), 0)
    used = jnp.concatenate(
        [((mask_ref[top : top + 1] >> point) & 1) * visible_ref[top : top + 1] for top in range(span)], axis=0
    )
    before = jnp.where(iota((pairs, pairs), 1) < iota((pairs, pairs), 0), 1.0, 0.0).astype(BF)
    place = jnp.dot(before, used.astype(F32).astype(BF), preferred_element_type=F32).astype(jnp.int32)
    place = jnp.where(used > 0, place, -1)
    count = jnp.sum(used, axis=0, keepdims=True)
    at = iota((pairs, columns), 0)
    column = iota((1, columns), 1)
    units = jnp.full((pairs, columns), pairs, jnp.int32)
    for pair in range(pairs):
        code = (column + pair // Q * columns) * 128 + pair
        units = jnp.where(place[pair : pair + 1] == at, code, units)
    units_ref[...] = jnp.concatenate([units, jnp.full((pairs, 128 - columns), pairs, jnp.int32)], axis=1)
    groups = jnp.maximum((count + GROUP - 1) // GROUP, 1)
    groups_ref[...] = jnp.concatenate([groups, jnp.full((1, 128 - columns), Q, jnp.int32)], axis=1)
    total_ref[...] = jnp.sum(groups, axis=1, keepdims=True)


def prepare_kernel(
    capacity, points_ref, weights_ref, normals_ref, visible_ref, mask_ref, across_ref, down_ref,
    total_ref, groups_ref, units_ref, slot_ref, gap_ref, depth_ref, face_ref,
):
    width = TS * Q
    span = normals_ref.shape[1] // TS
    iota = lambda shape, axis: lax.broadcasted_iota(jnp.int32, shape, axis)
    as_ones = lambda hit: jnp.where(hit, 1.0, 0.0).astype(BF)
    row = iota((width, 1), 0)
    order = as_ones(iota((width, width), 1) == (row % 8) * 64 + (row // 8 % 4) * Q + row // TS)
    same = as_ones(iota((width, width), 1) // Q == iota((width, width), 0) // Q)
    widen = as_ones(iota((TS, width), 1) // Q == iota((TS, width), 0))
    small = iota((TS, 1), 0)
    shuffle = as_ones(iota((TS, TS), 1) == (small % 8) * 4 + small // 8)
    across = ((1,), (1,))
    for top in range(span):
        at = slice(top * width, (top + 1) * width)
        x, y, z = (points_ref[k : k + 1, at] for k in range(3))
        weight = weights_ref[:, at]
        normal = normals_ref[:, top * TS : (top + 1) * TS]
        normal = jnp.concatenate([normal, jnp.zeros((5, TS), F32)], axis=0)
        high, middle, low = split(normal)
        face = jnp.concatenate([high, middle, low, high, middle, high], axis=0).astype(BF)
        face = lax.dot_general(shuffle, face, (across, ((), ())), preferred_element_type=F32)
        face_ref[top * TS : (top + 1) * TS] = face.astype(BF)
        wide = exact_dot((high, middle, low), widen)
        depth = wide[0:1] * x + wide[1:2] * y + wide[2:3] * z
        area = exact_dot(split(jnp.broadcast_to(weight, (8, width))), same)[0:1]
        scale = area / weight
        square = x * x + y * y + z * z + softening
        gap = by_rows((8, width), [-2.0 * x * scale, -2.0 * y * scale, -2.0 * z * scale, scale, square * scale])
        high, middle, low = split(gap)
        gap = jnp.concatenate([high, middle, low, high, middle, high], axis=0).astype(BF)
        gap = lax.dot_general(order, gap, (across, ((), ())), preferred_element_type=F32)
        gap_ref[top * Q : (top + 1) * Q] = gap.astype(BF).reshape(Q, TS, 48)
        parts = [jnp.broadcast_to(part, (128, width)).astype(BF) for part in split(depth)]
        deep = [lax.dot_general(order, part, (across, ((), ())), preferred_element_type=F32) for part in parts]
        depth_ref[top * Q : (top + 1) * Q] = (deep[0] + deep[1] + deep[2]).reshape(Q, TS, 128)
    list_work(visible_ref, mask_ref, across_ref, down_ref, capacity, total_ref, groups_ref, units_ref, slot_ref)
    gap_ref[span * Q] = jnp.where(iota((TS, 48), 1) == 4, 1.0, 0.0).astype(BF)
    depth_ref[span * Q] = jnp.zeros((TS, 128), F32)


def prepare(points, weights, normals, visible, quad_mask, owners, capacity):
    vmem = pl.BlockSpec(memory_space=pltpu.VMEM)
    pairs = normals.shape[1] // TS * Q
    tiles = owners.shape[0]
    whole = lambda *shape: jax.ShapeDtypeStruct(shape, jnp.int32)
    return pl.pallas_call(
        functools.partial(prepare_kernel, capacity),
        in_specs=[vmem] * 7,
        out_specs=[vmem] * 7,
        out_shape=[
            whole(1, 1),
            whole(1, 128),
            whole(pairs, 128),
            whole(1, tiles),
            jax.ShapeDtypeStruct((pairs + 1, TS, 48), BF),
            jax.ShapeDtypeStruct((pairs + 1, TS, 128), F32),
            jax.ShapeDtypeStruct((normals.shape[1], 48), BF),
        ],
        compiler_params=pltpu.CompilerParams(vmem_limit_bytes=40 * 2**20),
    )(points, weights, normals, visible, quad_mask, owners.reshape(1, tiles), owners.reshape(tiles, 1))


def column_features(packed_ref, rhs_ref, source):
    width = TS * Q
    span = rhs_ref.shape[0] // packed_ref.shape[0]
    for tile in range(span):
        base = span * Q + tile * 3
        nx, ny, nz = (packed_ref[source, base + k : base + k + 1] for k in range(3))
        for lanes in range(width // 128):
            at = tile * Q + lanes * 4
            x, y, z, w = (packed_ref[source, at + k : at + k + 1] for k in range(4))
            square = x * x + y * y + z * z
            depth = nx * x + ny * y + nz * z
            scale = w * (1.0 / math.pi)
            half = scale * -0.5
            ours = by_rows((8, 128), [x, y, z, square, jnp.ones_like(x)])
            theirs = by_rows((8, 128), [nx * half, ny * half, nz * half, -depth * scale])
            for block, start in ((ours, lanes * 128), (theirs, width + lanes * 128)):
                high, middle, low = split(block)
                rhs_ref[source * span + tile, :, start : start + 128] = jnp.concatenate(
                    [high, high, high, middle, middle, low], axis=0
                ).astype(BF)


def tiles_kernel(total_ref, groups_ref, units_ref, slot_ref, lhs_ref, depth_ref, face_ref, packed_ref, out_ref, acc, near, rhs_ref):
    out_ref[...] = jnp.zeros_like(out_ref)
    acc[...] = jnp.zeros_like(acc)
    width = TS * Q
    last = rhs_ref.shape[0] - 1

    def codes_of(place):
        tile, at = place
        return [units_ref[at * GROUP + g, tile] for g in range(GROUP)]

    def following(place):
        tile, at = place
        done = at + 1 >= groups_ref[0, tile]
        return (jnp.where(done, tile + 1, tile), jnp.where(done, 0, at + 1))

    def work_on(place):
        codes = codes_of(place)
        rows = [code % 128 for code in codes]
        tile = jnp.minimum(place[0], last)
        gap = jnp.concatenate([lhs_ref[r] for r in rows], axis=0)
        tops = [pl.ds(pl.multiple_of(jnp.minimum(r // Q, 3) * TS, TS), TS) for r in rows]
        total = [None] * GROUP
        for part in range(width // 256):
            at = slice(part * 256, (part + 1) * 256)
            ours = rhs_ref[tile, :, at]
            theirs = rhs_ref[tile, :, width + part * 256 : width + (part + 1) * 256]
            spread = jnp.dot(gap, ours, preferred_element_type=F32)
            cos_col = jnp.dot(gap, theirs, preferred_element_type=F32)
            value = jnp.maximum(cos_col, 0.0) * pl.reciprocal(spread * spread, approx=True)
            for g in range(GROUP):
                depth = depth_ref[rows[g]]
                for half in range(2):
                    lanes = slice(part * 256 + half * 128, part * 256 + (half + 1) * 128)
                    piece = jnp.maximum(near[tile, tops[g], lanes] - depth, 0.0) * value[g * TS : (g + 1) * TS, half * 128 : (half + 1) * 128]
                    total[g] = piece if total[g] is None else total[g] + piece
        return codes, total

    def some_groups(_, place):
        for _ in range(DEEP):
            codes, total = work_on(place)
            place = following(place)
            for g in range(GROUP):
                tile = codes[g] // 128
                acc[tile] = acc[tile] + total[g]
        return place

    def gather(source, _):
        column_features(packed_ref, rhs_ref, source)
        return 0

    lax.fori_loop(0, packed_ref.shape[0], gather, 0)

    def faces(step, _):
        for k in range(8):
            near[step * 8 + k] = jnp.dot(face_ref[...], rhs_ref[step * 8 + k, :, :width], preferred_element_type=F32)
        return 0

    lax.fori_loop(0, rhs_ref.shape[0] // 8, faces, 0)
    lax.fori_loop(0, (total_ref[0, 0] + DEEP - 1) // DEEP, some_groups, (jnp.int32(0), jnp.int32(0)))

    lane = lax.broadcasted_iota(jnp.int32, (8, 128), 1)
    second = (lane // TS) % 2 == 1
    upper = lane // (2 * TS) == 1

    def fold(step, _):
        for k in range(FOLD):
            tile = step * FOLD + k
            a0, a1, a2, a3 = [acc[tile, v * 8 : v * 8 + 8] for v in range(4)]
            low = jnp.where(second, a1, a0) + pltpu.roll(jnp.where(second, a0, a1), TS, 1)
            high = jnp.where(second, a3, a2) + pltpu.roll(jnp.where(second, a2, a3), TS, 1)
            mixed = jnp.where(upper, high, low) + pltpu.roll(jnp.where(upper, low, high), 2 * TS, 1)
            out_ref[slot_ref[0, tile]] = mixed
        return 0

    lax.fori_loop(0, acc.shape[0] // FOLD, fold, 0)


def assemble(total, groups, units, slot, lhs, depth, face, packed, slots):
    smem = pl.BlockSpec(memory_space=pltpu.SMEM)
    vmem = pl.BlockSpec(memory_space=pltpu.VMEM)
    tiles = slot.shape[1]
    columns = tiles * TS // face.shape[0]
    return pl.pallas_call(
        tiles_kernel,
        in_specs=[smem] * 4 + [vmem] * 4,
        out_specs=vmem,
        out_shape=jax.ShapeDtypeStruct((slots, 8, 128), F32),
        scratch_shapes=[
            pltpu.VMEM((tiles, TS, 128), F32),
            pltpu.VMEM((columns, face.shape[0], TS * Q), F32),
            pltpu.VMEM((columns, 48, 2 * TS * Q), BF),
        ],
        compiler_params=pltpu.CompilerParams(vmem_limit_bytes=56 * 2**20),
    )(total, groups, units, slot, lhs, depth, face, packed)


def pack_kernel(points_ref, weights_ref, normals_ref, out_ref, held):
    width = TS * Q
    span = normals_ref.shape[1] // TS
    lane = lax.broadcasted_iota(jnp.int32, (1, width), 1)
    wanted = (lane % TS) * Q + lane // TS
    order = jnp.where(lax.broadcasted_iota(jnp.int32, (width, width), 0) == wanted, 1.0, 0.0).astype(BF)
    rows = []
    for tile in range(span):
        at = slice(tile * width, (tile + 1) * width)
        rows += [points_ref[:, at], weights_ref[:, at]]
    rows = exact_dot(split(jnp.concatenate(rows, axis=0)), order)
    held[...] = jnp.zeros_like(held)
    for tile in range(span):
        for lanes in range(width // 128):
            at = tile * Q + lanes * 4
            held[at : at + 4] = rows[tile * 4 : tile * 4 + 4, lanes * 128 : (lanes + 1) * 128]
        normal = normals_ref[:, tile * TS : (tile + 1) * TS]
        at = span * Q + tile * 3
        held[at : at + 3] = jnp.concatenate([normal] * 4, axis=1)
    for receiver in range(out_ref.shape[0]):
        out_ref[receiver] = held[...]


def pack_columns(points, weights, normals, receivers):
    vmem = pl.BlockSpec(memory_space=pltpu.VMEM)
    rows = normals.shape[1] // TS * (Q + 3)
    rows += -rows % 8
    return pl.pallas_call(
        pack_kernel,
        in_specs=[vmem] * 3,
        out_specs=vmem,
        out_shape=jax.ShapeDtypeStruct((receivers, rows, 128), F32),
        scratch_shapes=[pltpu.VMEM((rows, 128), F32)],
        compiler_params=pltpu.CompilerParams(vmem_limit_bytes=40 * 2**20),
    )(points, weights, normals)


def on_device(points, normals, weights, visible, quad_mask, owners):
    devices = lax.axis_size("rows") * lax.axis_size("blk")
    sources = lax.axis_size("blk")
    capacity = max(2, 2 * owners.shape[1] // devices)
    weights = weights[None]
    spread = pack_columns(points, weights, normals, sources)
    gathered = lax.all_to_all(spread, "blk", split_axis=0, concat_axis=0, tiled=True)
    ready = prepare(points, weights, normals, visible, quad_mask, owners[0, :, 0], capacity)
    out = assemble(*ready, gathered, devices * capacity)
    arrived = lax.all_to_all(
        out.reshape(devices, capacity * 8, 128), ("rows", "blk"), split_axis=0, concat_axis=0, tiled=True
    )
    return arrived.reshape(devices * capacity, TS * TS)


def solution(mesh):
    placed = (
        P(None, ("rows", "blk")),
        P(None, ("rows", "blk")),
        P(("rows", "blk")),
        P(("rows", "blk"), None),
        P(("rows", "blk"), None),
        P(("rows", "blk"), None, None),
    )
    return jax.shard_map(
        on_device, mesh=mesh, in_specs=placed, out_specs=P(("rows", "blk"), None), check_vma=False
    )
```

```python
import functools
import math

import jax
import jax.numpy as jnp
from jax import lax
from jax.experimental import pallas as pl
from jax.experimental.pallas import tpu as pltpu
from jax.sharding import PartitionSpec as P

Q = 16
TS = 32
GROUP = 4
FOLD = 32
DEEP = 32
softening = 0.05
BF = jnp.bfloat16
F32 = jnp.float32


def split(x):
    high = x.astype(BF).astype(F32)
    rest = x - high
    middle = rest.astype(BF).astype(F32)
    return high, middle, rest - middle


def left_rows(four, last):
    high, middle, low = split(four)
    tail = jnp.concatenate(list(split(last)) + [jnp.zeros((5, four.shape[1]), F32)], axis=0)
    return jnp.concatenate([high, middle, low, high, middle, high, tail], axis=0).astype(BF)


def right_rows(twice, ones):
    high, middle, low = split(twice)
    upper = lax.broadcasted_iota(jnp.int32, twice.shape, 0) < 4
    blocks = [high, jnp.where(upper, high, middle), jnp.where(upper, middle, low), ones]
    return jnp.concatenate(blocks, axis=0).astype(BF)


def by_rows(shape, values, axis=0):
    at = lax.broadcasted_iota(jnp.int32, shape, axis)
    return functools.reduce(
        lambda acc, k: jnp.where(at == k, values[k], acc), range(len(values)), jnp.zeros(shape, F32)
    )


def exact_dot(parts, selector, contract=((1,), (0,))):
    dots = [lax.dot_general(part.astype(BF), selector, (contract, ((), ())), preferred_element_type=F32) for part in parts]
    return dots[0] + dots[1] + dots[2]


def list_work(visible_ref, mask_ref, across_ref, down_ref, capacity, total_ref, groups_ref, units_ref, slot_ref):
    span, columns = visible_ref.shape
    tiles = across_ref.shape[1]
    pairs = span * Q
    iota = lambda shape, axis: lax.broadcasted_iota(jnp.int32, shape, axis)
    earlier = (across_ref[...] == down_ref[...]) & (iota((tiles, tiles), 0) < iota((tiles, tiles), 1))
    rank = jnp.sum(jnp.where(earlier, 1, 0), axis=0, keepdims=True)
    slot_ref[...] = across_ref[...] * capacity + rank
    point = iota((Q, columns), 0)
    used = jnp.concatenate(
        [((mask_ref[top : top + 1] >> point) & 1) * visible_ref[top : top + 1] for top in range(span)], axis=0
    )
    before = jnp.where(iota((pairs, pairs), 1) < iota((pairs, pairs), 0), 1.0, 0.0).astype(BF)
    place = jnp.dot(before, used.astype(F32).astype(BF), preferred_element_type=F32).astype(jnp.int32)
    place = jnp.where(used > 0, place, -1)
    count = jnp.sum(used, axis=0, keepdims=True)
    at = iota((pairs, columns), 0)
    column = iota((1, columns), 1)
    units = jnp.full((pairs, columns), pairs, jnp.int32)
    for pair in range(pairs):
        code = (column + pair // Q * columns) * 128 + pair
        units = jnp.where(place[pair : pair + 1] == at, code, units)
    units_ref[...] = jnp.concatenate([units, jnp.full((pairs, 128 - columns), pairs, jnp.int32)], axis=1)
    groups = jnp.maximum((count + GROUP - 1) // GROUP, 1)
    groups_ref[...] = jnp.concatenate([groups, jnp.full((1, 128 - columns), Q, jnp.int32)], axis=1)
    total_ref[...] = jnp.sum(groups, axis=1, keepdims=True)


def prepare_kernel(
    capacity, points_ref, weights_ref, normals_ref, visible_ref, mask_ref, across_ref, down_ref,
    total_ref, groups_ref, units_ref, slot_ref, gap_ref, depth_ref, face_ref,
):
    width = TS * Q
    span = normals_ref.shape[1] // TS
    iota = lambda shape, axis: lax.broadcasted_iota(jnp.int32, shape, axis)
    as_ones = lambda hit: jnp.where(hit, 1.0, 0.0).astype(BF)
    row = iota((width, 1), 0)
    order = as_ones(iota((width, width), 1) == (row % 8) * 64 + (row // 8 % 4) * Q + row // TS)
    same = as_ones(iota((width, width), 1) // Q == iota((width, width), 0) // Q)
    widen = as_ones(iota((TS, width), 1) // Q == iota((TS, width), 0))
    small = iota((TS, 1), 0)
    shuffle = as_ones(iota((TS, TS), 1) == (small % 8) * 4 + small // 8)
    across = ((1,), (1,))
    for top in range(span):
        at = slice(top * width, (top + 1) * width)
        x, y, z = (points_ref[k : k + 1, at] for k in range(3))
        weight = weights_ref[:, at]
        normal = normals_ref[:, top * TS : (top + 1) * TS]
        normal = jnp.concatenate([normal, jnp.zeros((1, TS), F32)], axis=0)
        face = left_rows(normal, jnp.zeros((1, TS), F32))
        face = lax.dot_general(shuffle, face, (across, ((), ())), preferred_element_type=F32)
        face_ref[top * TS : (top + 1) * TS] = face.astype(BF)
        wide = exact_dot(split(normal), widen)
        depth = wide[0:1] * x + wide[1:2] * y + wide[2:3] * z
        area = exact_dot(split(jnp.broadcast_to(weight, (8, width))), same)[0:1]
        scale = area / weight
        square = x * x + y * y + z * z + softening
        gap = jnp.concatenate([-2.0 * x * scale, -2.0 * y * scale, -2.0 * z * scale, scale], axis=0)
        gap = left_rows(gap, square * scale)
        gap = lax.dot_general(order, gap, (across, ((), ())), preferred_element_type=F32)
        gap_ref[top * Q : (top + 1) * Q] = gap.astype(BF).reshape(Q, TS, 32)
        parts = [jnp.broadcast_to(part, (128, width)).astype(BF) for part in split(depth)]
        deep = [lax.dot_general(order, part, (across, ((), ())), preferred_element_type=F32) for part in parts]
        depth_ref[top * Q : (top + 1) * Q] = (deep[0] + deep[1] + deep[2]).reshape(Q, TS, 128)
    list_work(visible_ref, mask_ref, across_ref, down_ref, capacity, total_ref, groups_ref, units_ref, slot_ref)
    gap_ref[span * Q] = jnp.where(iota((TS, 32), 1) == 24, 1.0, 0.0).astype(BF)
    depth_ref[span * Q] = jnp.zeros((TS, 128), F32)


def prepare(points, weights, normals, visible, quad_mask, owners, capacity):
    vmem = pl.BlockSpec(memory_space=pltpu.VMEM)
    pairs = normals.shape[1] // TS * Q
    tiles = owners.shape[0]
    whole = lambda *shape: jax.ShapeDtypeStruct(shape, jnp.int32)
    return pl.pallas_call(
        functools.partial(prepare_kernel, capacity),
        in_specs=[vmem] * 7,
        out_specs=[vmem] * 7,
        out_shape=[
            whole(1, 1),
            whole(1, 128),
            whole(pairs, 128),
            whole(1, tiles),
            jax.ShapeDtypeStruct((pairs + 1, TS, 32), BF),
            jax.ShapeDtypeStruct((pairs + 1, TS, 128), F32),
            jax.ShapeDtypeStruct((normals.shape[1], 32), BF),
        ],
        compiler_params=pltpu.CompilerParams(vmem_limit_bytes=60 * 2**20),
    )(points, weights, normals, visible, quad_mask, owners.reshape(1, tiles), owners.reshape(tiles, 1))


def column_features(packed_ref, rhs_ref, source):
    width = TS * Q
    span = rhs_ref.shape[0] // packed_ref.shape[0]
    ones = jnp.where(lax.broadcasted_iota(jnp.int32, (8, 128), 0) < 3, 1.0, 0.0)
    for tile in range(span):
        base = span * Q + tile * 3
        nx, ny, nz = (packed_ref[source, base + k : base + k + 1] for k in range(3))
        for lanes in range(width // 128):
            at = tile * Q + lanes * 4
            x, y, z, w = (packed_ref[source, at + k : at + k + 1] for k in range(4))
            square = x * x + y * y + z * z
            depth = nx * x + ny * y + nz * z
            scale = w * (1.0 / math.pi)
            half = scale * -0.5
            four = [x, y, z, square]
            rhs_ref[source * span + tile, :, lanes * 128 : (lanes + 1) * 128] = right_rows(by_rows((8, 128), four + four), ones)
            four = [nx * half, ny * half, nz * half, -depth * scale]
            start = width + lanes * 128
            rhs_ref[source * span + tile, :, start : start + 128] = right_rows(by_rows((8, 128), four + four), ones * 0.0)


def tiles_kernel(total_ref, groups_ref, units_ref, slot_ref, lhs_ref, depth_ref, face_ref, packed_ref, out_ref, acc, near, rhs_ref):
    out_ref[...] = jnp.zeros_like(out_ref)
    acc[...] = jnp.zeros_like(acc)
    width = TS * Q
    last = rhs_ref.shape[0] - 1

    def codes_of(place):
        tile, at = place
        return [units_ref[at * GROUP + g, tile] for g in range(GROUP)]

    def following(place):
        tile, at = place
        done = at + 1 >= groups_ref[0, tile]
        return (jnp.where(done, tile + 1, tile), jnp.where(done, 0, at + 1))

    def work_on(place):
        codes = codes_of(place)
        rows = [code % 128 for code in codes]
        tile = jnp.minimum(place[0], last)
        gap = jnp.concatenate([lhs_ref[r] for r in rows], axis=0)
        tops = [pl.ds(pl.multiple_of(jnp.minimum(r // Q, 3) * TS, TS), TS) for r in rows]
        total = [None] * GROUP
        for part in range(width // 256):
            at = slice(part * 256, (part + 1) * 256)
            ours = rhs_ref[tile, :, at]
            theirs = rhs_ref[tile, :, width + part * 256 : width + (part + 1) * 256]
            spread = jnp.dot(gap, ours, preferred_element_type=F32)
            cos_col = jnp.dot(gap, theirs, preferred_element_type=F32)
            value = jnp.maximum(cos_col, 0.0) * pl.reciprocal(spread * spread, approx=True)
            for g in range(GROUP):
                depth = depth_ref[rows[g]]
                for half in range(2):
                    lanes = slice(part * 256 + half * 128, part * 256 + (half + 1) * 128)
                    piece = jnp.maximum(near[tile, tops[g], lanes] - depth, 0.0) * value[g * TS : (g + 1) * TS, half * 128 : (half + 1) * 128]
                    total[g] = piece if total[g] is None else total[g] + piece
        return codes, total

    def some_groups(_, place):
        for _ in range(DEEP):
            codes, total = work_on(place)
            place = following(place)
            for g in range(GROUP):
                tile = codes[g] // 128
                acc[tile] = acc[tile] + total[g]
        return place

    def gather(source, _):
        column_features(packed_ref, rhs_ref, source)
        return 0

    lax.fori_loop(0, packed_ref.shape[0], gather, 0)

    def faces(step, _):
        for k in range(8):
            near[step * 8 + k] = jnp.dot(face_ref[...], rhs_ref[step * 8 + k, :, :width], preferred_element_type=F32)
        return 0

    lax.fori_loop(0, rhs_ref.shape[0] // 8, faces, 0)
    lax.fori_loop(0, (total_ref[0, 0] + DEEP - 1) // DEEP, some_groups, (jnp.int32(0), jnp.int32(0)))

    lane = lax.broadcasted_iota(jnp.int32, (8, 128), 1)
    second = (lane // TS) % 2 == 1
    upper = lane // (2 * TS) == 1

    def fold(step, _):
        for k in range(FOLD):
            tile = step * FOLD + k
            a0, a1, a2, a3 = [acc[tile, v * 8 : v * 8 + 8] for v in range(4)]
            low = jnp.where(second, a1, a0) + pltpu.roll(jnp.where(second, a0, a1), TS, 1)
            high = jnp.where(second, a3, a2) + pltpu.roll(jnp.where(second, a2, a3), TS, 1)
            mixed = jnp.where(upper, high, low) + pltpu.roll(jnp.where(upper, low, high), 2 * TS, 1)
            out_ref[slot_ref[0, tile]] = mixed
        return 0

    lax.fori_loop(0, acc.shape[0] // FOLD, fold, 0)


def assemble(total, groups, units, slot, lhs, depth, face, packed, slots):
    smem = pl.BlockSpec(memory_space=pltpu.SMEM)
    vmem = pl.BlockSpec(memory_space=pltpu.VMEM)
    tiles = slot.shape[1]
    columns = tiles * TS // face.shape[0]
    return pl.pallas_call(
        tiles_kernel,
        in_specs=[smem] * 4 + [vmem] * 4,
        out_specs=vmem,
        out_shape=jax.ShapeDtypeStruct((slots, 8, 128), F32),
        scratch_shapes=[
            pltpu.VMEM((tiles, TS, 128), F32),
            pltpu.VMEM((columns, face.shape[0], TS * Q), F32),
            pltpu.VMEM((columns, 32, 2 * TS * Q), BF),
        ],
        compiler_params=pltpu.CompilerParams(vmem_limit_bytes=60 * 2**20),
    )(total, groups, units, slot, lhs, depth, face, packed)


def pack_kernel(points_ref, weights_ref, normals_ref, out_ref, held):
    width = TS * Q
    span = normals_ref.shape[1] // TS
    lane = lax.broadcasted_iota(jnp.int32, (1, width), 1)
    wanted = (lane % TS) * Q + lane // TS
    order = jnp.where(lax.broadcasted_iota(jnp.int32, (width, width), 0) == wanted, 1.0, 0.0).astype(BF)
    rows = []
    for tile in range(span):
        at = slice(tile * width, (tile + 1) * width)
        rows += [points_ref[:, at], weights_ref[:, at]]
    rows = exact_dot(split(jnp.concatenate(rows, axis=0)), order)
    held[...] = jnp.zeros_like(held)
    for tile in range(span):
        for lanes in range(width // 128):
            at = tile * Q + lanes * 4
            held[at : at + 4] = rows[tile * 4 : tile * 4 + 4, lanes * 128 : (lanes + 1) * 128]
        normal = normals_ref[:, tile * TS : (tile + 1) * TS]
        at = span * Q + tile * 3
        held[at : at + 3] = jnp.concatenate([normal] * 4, axis=1)
    for receiver in range(out_ref.shape[0]):
        out_ref[receiver] = held[...]


def pack_columns(points, weights, normals, receivers):
    vmem = pl.BlockSpec(memory_space=pltpu.VMEM)
    rows = normals.shape[1] // TS * (Q + 3)
    rows += -rows % 8
    return pl.pallas_call(
        pack_kernel,
        in_specs=[vmem] * 3,
        out_specs=vmem,
        out_shape=jax.ShapeDtypeStruct((receivers, rows, 128), F32),
        scratch_shapes=[pltpu.VMEM((rows, 128), F32)],
        compiler_params=pltpu.CompilerParams(vmem_limit_bytes=60 * 2**20),
    )(points, weights, normals)


def on_device(points, normals, weights, visible, quad_mask, owners):
    devices = lax.axis_size("rows") * lax.axis_size("blk")
    sources = lax.axis_size("blk")
    capacity = max(2, 2 * owners.shape[1] // devices)
    weights = weights[None]
    spread = pack_columns(points, weights, normals, sources)
    gathered = lax.all_to_all(spread, "blk", split_axis=0, concat_axis=0, tiled=True)
    ready = prepare(points, weights, normals, visible, quad_mask, owners[0, :, 0], capacity)
    out = assemble(*ready, gathered, devices * capacity)
    arrived = lax.all_to_all(
        out.reshape(devices, capacity * 8, 128), ("rows", "blk"), split_axis=0, concat_axis=0, tiled=True
    )
    return arrived.reshape(devices * capacity, TS * TS)


def solution(mesh):
    placed = (
        P(None, ("rows", "blk")),
        P(None, ("rows", "blk")),
        P(("rows", "blk")),
        P(("rows", "blk"), None),
        P(("rows", "blk"), None),
        P(("rows", "blk"), None, None),
    )
    return jax.shard_map(
        on_device, mesh=mesh, in_specs=placed, out_specs=P(("rows", "blk"), None), check_vma=False
    )
```

```python
import functools
import math

import jax
import jax.numpy as jnp
from jax import lax
from jax.experimental import pallas as pl
from jax.experimental.pallas import tpu as pltpu
from jax.sharding import PartitionSpec as P

Q = 16
TS = 32
GROUP = 4
FOLD = 32
DEEP = 64
REST = 8
softening = 0.05
BF = jnp.bfloat16
F32 = jnp.float32


def split(x):
    high = x.astype(BF).astype(F32)
    rest = x - high
    middle = rest.astype(BF).astype(F32)
    return high, middle, rest - middle


def left_rows(four, last):
    high, middle, low = split(four)
    tail = jnp.concatenate(list(split(last)) + [jnp.zeros((5, four.shape[1]), F32)], axis=0)
    return jnp.concatenate([high, middle, low, high, middle, high, tail], axis=0).astype(BF)


def right_rows(twice, ones):
    high, middle, low = split(twice)
    upper = lax.broadcasted_iota(jnp.int32, twice.shape, 0) < 4
    blocks = [high, jnp.where(upper, high, middle), jnp.where(upper, middle, low), ones]
    return jnp.concatenate(blocks, axis=0).astype(BF)


def by_rows(shape, values, axis=0):
    at = lax.broadcasted_iota(jnp.int32, shape, axis)
    return functools.reduce(
        lambda acc, k: jnp.where(at == k, values[k], acc), range(len(values)), jnp.zeros(shape, F32)
    )


def exact_dot(parts, selector, contract=((1,), (0,))):
    dots = [lax.dot_general(part.astype(BF), selector, (contract, ((), ())), preferred_element_type=F32) for part in parts]
    return dots[0] + dots[1] + dots[2]


def list_work(visible_ref, mask_ref, across_ref, down_ref, capacity, total_ref, groups_ref, units_ref, slot_ref):
    span, columns = visible_ref.shape
    tiles = across_ref.shape[1]
    pairs = span * Q
    iota = lambda shape, axis: lax.broadcasted_iota(jnp.int32, shape, axis)
    earlier = (across_ref[...] == down_ref[...]) & (iota((tiles, tiles), 0) < iota((tiles, tiles), 1))
    rank = jnp.sum(jnp.where(earlier, 1, 0), axis=0, keepdims=True)
    slot_ref[...] = across_ref[...] * capacity + rank
    point = iota((Q, columns), 0)
    used = jnp.concatenate(
        [((mask_ref[top : top + 1] >> point) & 1) * visible_ref[top : top + 1] for top in range(span)], axis=0
    )
    before = jnp.where(iota((pairs, pairs), 1) < iota((pairs, pairs), 0), 1.0, 0.0).astype(BF)
    place = jnp.dot(before, used.astype(F32).astype(BF), preferred_element_type=F32).astype(jnp.int32)
    place = jnp.where(used > 0, place, -1)
    count = jnp.sum(used, axis=0, keepdims=True)
    at = iota((pairs, columns), 0)
    column = iota((1, columns), 1)
    units = jnp.full((pairs, columns), pairs, jnp.int32)
    for pair in range(pairs):
        code = (column + pair // Q * columns) * 128 + pair
        units = jnp.where(place[pair : pair + 1] == at, code, units)
    units_ref[...] = jnp.concatenate([units, jnp.full((pairs, 128 - columns), pairs, jnp.int32)], axis=1)
    groups = jnp.maximum((count + GROUP - 1) // GROUP, 1)
    groups_ref[...] = jnp.concatenate([groups, jnp.full((1, 128 - columns), Q, jnp.int32)], axis=1)
    total_ref[...] = jnp.sum(groups, axis=1, keepdims=True)


def prepare_kernel(
    capacity, points_ref, weights_ref, normals_ref, visible_ref, mask_ref, across_ref, down_ref,
    total_ref, groups_ref, units_ref, slot_ref, gap_ref, depth_ref, face_ref,
):
    width = TS * Q
    span = normals_ref.shape[1] // TS
    iota = lambda shape, axis: lax.broadcasted_iota(jnp.int32, shape, axis)
    as_ones = lambda hit: jnp.where(hit, 1.0, 0.0).astype(BF)
    row = iota((width, 1), 0)
    order = as_ones(iota((width, width), 1) == (row % 8) * 64 + (row // 8 % 4) * Q + row // TS)
    same = as_ones(iota((width, width), 1) // Q == iota((width, width), 0) // Q)
    widen = as_ones(iota((TS, width), 1) // Q == iota((TS, width), 0))
    small = iota((TS, 1), 0)
    shuffle = as_ones(iota((TS, TS), 1) == (small % 8) * 4 + small // 8)
    across = ((1,), (1,))
    for top in range(span):
        at = slice(top * width, (top + 1) * width)
        x, y, z = (points_ref[k : k + 1, at] for k in range(3))
        weight = weights_ref[:, at]
        normal = normals_ref[:, top * TS : (top + 1) * TS]
        normal = jnp.concatenate([normal, jnp.zeros((1, TS), F32)], axis=0)
        face = left_rows(normal, jnp.zeros((1, TS), F32))
        face = lax.dot_general(shuffle, face, (across, ((), ())), preferred_element_type=F32)
        face_ref[top * TS : (top + 1) * TS] = face.astype(BF)
        wide = exact_dot(split(normal), widen)
        depth = wide[0:1] * x + wide[1:2] * y + wide[2:3] * z
        area = exact_dot(split(jnp.broadcast_to(weight, (8, width))), same)[0:1]
        scale = area / weight
        square = x * x + y * y + z * z + softening
        gap = jnp.concatenate([-2.0 * x * scale, -2.0 * y * scale, -2.0 * z * scale, scale], axis=0)
        gap = left_rows(gap, square * scale)
        gap = lax.dot_general(order, gap, (across, ((), ())), preferred_element_type=F32)
        gap_ref[top * Q : (top + 1) * Q] = gap.astype(BF).reshape(Q, TS, 32)
        parts = [jnp.broadcast_to(part, (128, width)).astype(BF) for part in split(depth)]
        deep = [lax.dot_general(order, part, (across, ((), ())), preferred_element_type=F32) for part in parts]
        depth_ref[top * Q : (top + 1) * Q] = (deep[0] + deep[1] + deep[2]).reshape(Q, TS, 128)
    list_work(visible_ref, mask_ref, across_ref, down_ref, capacity, total_ref, groups_ref, units_ref, slot_ref)
    gap_ref[span * Q] = jnp.where(iota((TS, 32), 1) == 24, 1.0, 0.0).astype(BF)
    depth_ref[span * Q] = jnp.zeros((TS, 128), F32)


def prepare(points, weights, normals, visible, quad_mask, owners, capacity):
    vmem = pl.BlockSpec(memory_space=pltpu.VMEM)
    pairs = normals.shape[1] // TS * Q
    tiles = owners.shape[0]
    whole = lambda *shape: jax.ShapeDtypeStruct(shape, jnp.int32)
    return pl.pallas_call(
        functools.partial(prepare_kernel, capacity),
        in_specs=[vmem] * 7,
        out_specs=[vmem] * 7,
        out_shape=[
            whole(1, 1),
            whole(1, 128),
            whole(pairs, 128),
            whole(1, tiles),
            jax.ShapeDtypeStruct((pairs + 1, TS, 32), BF),
            jax.ShapeDtypeStruct((pairs + 1, TS, 128), F32),
            jax.ShapeDtypeStruct((normals.shape[1], 32), BF),
        ],
        compiler_params=pltpu.CompilerParams(vmem_limit_bytes=60 * 2**20),
    )(points, weights, normals, visible, quad_mask, owners.reshape(1, tiles), owners.reshape(tiles, 1))


def column_features(packed_ref, rhs_ref, source):
    width = TS * Q
    span = rhs_ref.shape[0] // packed_ref.shape[0]
    ones = jnp.where(lax.broadcasted_iota(jnp.int32, (8, 128), 0) < 3, 1.0, 0.0)
    for tile in range(span):
        base = span * Q + tile * 3
        nx, ny, nz = (packed_ref[source, base + k : base + k + 1] for k in range(3))
        for lanes in range(width // 128):
            at = tile * Q + lanes * 4
            x, y, z, w = (packed_ref[source, at + k : at + k + 1] for k in range(4))
            square = x * x + y * y + z * z
            depth = nx * x + ny * y + nz * z
            scale = w * (1.0 / math.pi)
            half = scale * -0.5
            four = [x, y, z, square]
            rhs_ref[source * span + tile, :, lanes * 128 : (lanes + 1) * 128] = right_rows(by_rows((8, 128), four + four), ones)
            four = [nx * half, ny * half, nz * half, -depth * scale]
            start = width + lanes * 128
            rhs_ref[source * span + tile, :, start : start + 128] = right_rows(by_rows((8, 128), four + four), ones * 0.0)


def tiles_kernel(
    total_ref, groups_ref, units_ref, slot_ref, lhs_hbm, depth_hbm, face_hbm, packed_hbm, out_ref,
    acc, near, rhs_ref, lhs_ref, depth_ref, face_ref, packed_ref, arrived,
):
    far = (packed_hbm, face_hbm, lhs_hbm, depth_hbm)
    copies = [
        pltpu.make_async_copy(source, target, arrived.at[k])
        for k, (source, target) in enumerate(zip(far, (packed_ref, face_ref, lhs_ref, depth_ref)))
    ]
    for copy in copies:
        copy.start()
    out_ref[...] = jnp.zeros_like(out_ref)
    acc[...] = jnp.zeros_like(acc)
    width = TS * Q
    last = rhs_ref.shape[0] - 1

    def codes_of(place):
        tile, at = place
        return [units_ref[at * GROUP + g, tile] for g in range(GROUP)]

    def following(place):
        tile, at = place
        done = at + 1 >= groups_ref[0, tile]
        return (jnp.where(done, tile + 1, tile), jnp.where(done, 0, at + 1))

    def work_on(place):
        codes = codes_of(place)
        rows = [code % 128 for code in codes]
        tile = jnp.minimum(place[0], last)
        gap = jnp.concatenate([lhs_ref[r] for r in rows], axis=0)
        tops = [pl.ds(pl.multiple_of(jnp.minimum(r // Q, 3) * TS, TS), TS) for r in rows]
        total = [None] * GROUP
        for part in range(width // 256):
            at = slice(part * 256, (part + 1) * 256)
            ours = rhs_ref[tile, :, at]
            theirs = rhs_ref[tile, :, width + part * 256 : width + (part + 1) * 256]
            spread = jnp.dot(gap, ours, preferred_element_type=F32)
            cos_col = jnp.dot(gap, theirs, preferred_element_type=F32)
            value = jnp.maximum(cos_col, 0.0) * pl.reciprocal(spread * spread, approx=True)
            for g in range(GROUP):
                depth = depth_ref[rows[g]]
                for half in range(2):
                    lanes = slice(part * 256 + half * 128, part * 256 + (half + 1) * 128)
                    piece = jnp.maximum(near[tile, tops[g], lanes] - depth, 0.0) * value[g * TS : (g + 1) * TS, half * 128 : (half + 1) * 128]
                    total[g] = piece if total[g] is None else total[g] + piece
        return codes, total

    def some_groups(count):
        def run(_, place):
            for _ in range(count):
                codes, total = work_on(place)
                place = following(place)
                for g in range(GROUP):
                    tile = codes[g] // 128
                    acc[tile] = acc[tile] + total[g]
            return place

        return run

    def gather(source, _):
        column_features(packed_ref, rhs_ref, source)
        return 0

    copies[0].wait()
    lax.fori_loop(0, packed_ref.shape[0], gather, 0)

    def faces(step, _):
        for k in range(8):
            near[step * 8 + k] = jnp.dot(face_ref[...], rhs_ref[step * 8 + k, :, :width], preferred_element_type=F32)
        return 0

    copies[1].wait()
    lax.fori_loop(0, rhs_ref.shape[0] // 8, faces, 0)
    copies[2].wait()
    copies[3].wait()
    whole = total_ref[0, 0] // DEEP
    rest = total_ref[0, 0] - whole * DEEP
    place = lax.fori_loop(0, whole, some_groups(DEEP), (jnp.int32(0), jnp.int32(0)))
    lax.fori_loop(0, (rest + REST - 1) // REST, some_groups(REST), place)

    lane = lax.broadcasted_iota(jnp.int32, (8, 128), 1)
    second = (lane // TS) % 2 == 1
    upper = lane // (2 * TS) == 1

    def fold(step, _):
        for k in range(FOLD):
            tile = step * FOLD + k
            a0, a1, a2, a3 = [acc[tile, v * 8 : v * 8 + 8] for v in range(4)]
            low = jnp.where(second, a1, a0) + pltpu.roll(jnp.where(second, a0, a1), TS, 1)
            high = jnp.where(second, a3, a2) + pltpu.roll(jnp.where(second, a2, a3), TS, 1)
            mixed = jnp.where(upper, high, low) + pltpu.roll(jnp.where(upper, low, high), 2 * TS, 1)
            out_ref[slot_ref[0, tile]] = mixed
        return 0

    lax.fori_loop(0, acc.shape[0] // FOLD, fold, 0)


def assemble(total, groups, units, slot, lhs, depth, face, packed, slots):
    smem = pl.BlockSpec(memory_space=pltpu.SMEM)
    vmem = pl.BlockSpec(memory_space=pltpu.VMEM)
    tiles = slot.shape[1]
    columns = tiles * TS // face.shape[0]
    return pl.pallas_call(
        tiles_kernel,
        in_specs=[smem] * 4 + [pl.BlockSpec(memory_space=pl.ANY)] * 4,
        out_specs=vmem,
        out_shape=jax.ShapeDtypeStruct((slots, 8, 128), F32),
        scratch_shapes=[
            pltpu.VMEM((tiles, TS, 128), F32),
            pltpu.VMEM((columns, face.shape[0], TS * Q), F32),
            pltpu.VMEM((columns, 32, 2 * TS * Q), BF),
            pltpu.VMEM(lhs.shape, BF),
            pltpu.VMEM(depth.shape, F32),
            pltpu.VMEM(face.shape, BF),
            pltpu.VMEM(packed.shape, F32),
            pltpu.SemaphoreType.DMA((4,)),
        ],
        compiler_params=pltpu.CompilerParams(vmem_limit_bytes=60 * 2**20),
    )(total, groups, units, slot, lhs, depth, face, packed)


def pack_kernel(points_ref, weights_ref, normals_ref, out_ref, held):
    width = TS * Q
    span = normals_ref.shape[1] // TS
    lane = lax.broadcasted_iota(jnp.int32, (1, width), 1)
    wanted = (lane % TS) * Q + lane // TS
    order = jnp.where(lax.broadcasted_iota(jnp.int32, (width, width), 0) == wanted, 1.0, 0.0).astype(BF)
    rows = []
    for tile in range(span):
        at = slice(tile * width, (tile + 1) * width)
        rows += [points_ref[:, at], weights_ref[:, at]]
    rows = exact_dot(split(jnp.concatenate(rows, axis=0)), order)
    held[...] = jnp.zeros_like(held)
    for tile in range(span):
        for lanes in range(width // 128):
            at = tile * Q + lanes * 4
            held[at : at + 4] = rows[tile * 4 : tile * 4 + 4, lanes * 128 : (lanes + 1) * 128]
        normal = normals_ref[:, tile * TS : (tile + 1) * TS]
        at = span * Q + tile * 3
        held[at : at + 3] = jnp.concatenate([normal] * 4, axis=1)
    for receiver in range(out_ref.shape[0]):
        out_ref[receiver] = held[...]


def pack_columns(points, weights, normals, receivers):
    vmem = pl.BlockSpec(memory_space=pltpu.VMEM)
    rows = normals.shape[1] // TS * (Q + 3)
    rows += -rows % 8
    return pl.pallas_call(
        pack_kernel,
        in_specs=[vmem] * 3,
        out_specs=vmem,
        out_shape=jax.ShapeDtypeStruct((receivers, rows, 128), F32),
        scratch_shapes=[pltpu.VMEM((rows, 128), F32)],
        compiler_params=pltpu.CompilerParams(vmem_limit_bytes=60 * 2**20),
    )(points, weights, normals)


def on_device(points, normals, weights, visible, quad_mask, owners):
    devices = lax.axis_size("rows") * lax.axis_size("blk")
    sources = lax.axis_size("blk")
    capacity = max(2, 2 * owners.shape[1] // devices)
    weights = weights[None]
    spread = pack_columns(points, weights, normals, sources)
    gathered = lax.all_to_all(spread, "blk", split_axis=0, concat_axis=0, tiled=True)
    ready = prepare(points, weights, normals, visible, quad_mask, owners[0, :, 0], capacity)
    out = assemble(*ready, gathered, devices * capacity)
    arrived = lax.all_to_all(
        out.reshape(devices, capacity * 8, 128), ("rows", "blk"), split_axis=0, concat_axis=0, tiled=True
    )
    return arrived.reshape(devices * capacity, TS * TS)


def solution(mesh):
    placed = (
        P(None, ("rows", "blk")),
        P(None, ("rows", "blk")),
        P(("rows", "blk")),
        P(("rows", "blk"), None),
        P(("rows", "blk"), None),
        P(("rows", "blk"), None, None),
    )
    return jax.shard_map(
        on_device, mesh=mesh, in_specs=placed, out_specs=P(("rows", "blk"), None), check_vma=False
    )
```

```python
import functools
import math

import jax
import jax.numpy as jnp
from jax import lax
from jax.experimental import pallas as pl
from jax.experimental.pallas import tpu as pltpu
from jax.sharding import PartitionSpec as P

Q = 16
TS = 32
GROUP = 4
FOLD = 32
DEEP = 64
REST = 8
softening = 0.05
BF = jnp.bfloat16
F32 = jnp.float32


def split(x):
    high = x.astype(BF).astype(F32)
    rest = x - high
    middle = rest.astype(BF).astype(F32)
    return high, middle, rest - middle


def left_rows(four, last):
    high, middle, low = split(four)
    tail = jnp.concatenate(list(split(last)) + [jnp.zeros((5, four.shape[1]), F32)], axis=0)
    return jnp.concatenate([high, middle, low, high, middle, high, tail], axis=0).astype(BF)


def right_rows(twice, ones):
    high, middle, low = split(twice)
    upper = lax.broadcasted_iota(jnp.int32, twice.shape, 0) < 4
    blocks = [high, jnp.where(upper, high, middle), jnp.where(upper, middle, low), ones]
    return jnp.concatenate(blocks, axis=0).astype(BF)


def by_rows(shape, values, axis=0):
    at = lax.broadcasted_iota(jnp.int32, shape, axis)
    return functools.reduce(
        lambda acc, k: jnp.where(at == k, values[k], acc), range(len(values)), jnp.zeros(shape, F32)
    )


def exact_dot(parts, selector, contract=((1,), (0,))):
    dots = [lax.dot_general(part.astype(BF), selector, (contract, ((), ())), preferred_element_type=F32) for part in parts]
    return dots[0] + dots[1] + dots[2]


def list_work(visible_ref, mask_ref, across_ref, down_ref, capacity, total_ref, groups_ref, units_ref, slot_ref):
    span, columns = visible_ref.shape
    tiles = across_ref.shape[1]
    pairs = span * Q
    iota = lambda shape, axis: lax.broadcasted_iota(jnp.int32, shape, axis)
    earlier = (across_ref[...] == down_ref[...]) & (iota((tiles, tiles), 0) < iota((tiles, tiles), 1))
    rank = jnp.sum(jnp.where(earlier, 1, 0), axis=0, keepdims=True)
    slot_ref[...] = across_ref[...] * capacity + rank
    point = iota((Q, columns), 0)
    used = jnp.concatenate(
        [((mask_ref[top : top + 1] >> point) & 1) * visible_ref[top : top + 1] for top in range(span)], axis=0
    )
    before = jnp.where(iota((pairs, pairs), 1) < iota((pairs, pairs), 0), 1.0, 0.0).astype(BF)
    place = jnp.dot(before, used.astype(F32).astype(BF), preferred_element_type=F32).astype(jnp.int32)
    place = jnp.where(used > 0, place, -1)
    count = jnp.sum(used, axis=0, keepdims=True)
    at = iota((pairs, columns), 0)
    column = iota((1, columns), 1)
    units = jnp.full((pairs, columns), pairs, jnp.int32)
    for pair in range(pairs):
        code = (column + pair // Q * columns) * 128 + pair
        units = jnp.where(place[pair : pair + 1] == at, code, units)
    units_ref[...] = jnp.concatenate([units, jnp.full((pairs, 128 - columns), pairs, jnp.int32)], axis=1)
    groups = jnp.maximum((count + GROUP - 1) // GROUP, 1)
    groups_ref[...] = jnp.concatenate([groups, jnp.full((1, 128 - columns), Q, jnp.int32)], axis=1)
    total_ref[...] = jnp.sum(groups, axis=1, keepdims=True)


def prepare_kernel(
    capacity, points_ref, weights_ref, normals_ref, visible_ref, mask_ref, across_ref, down_ref,
    total_ref, groups_ref, units_ref, slot_ref, gap_ref, depth_ref, face_ref,
):
    width = TS * Q
    span = normals_ref.shape[1] // TS
    iota = lambda shape, axis: lax.broadcasted_iota(jnp.int32, shape, axis)
    as_ones = lambda hit: jnp.where(hit, 1.0, 0.0).astype(BF)
    row = iota((width, 1), 0)
    order = as_ones(iota((width, width), 1) == (row % 8) * 64 + (row // 8 % 4) * Q + row // TS)
    same = as_ones(iota((width, width), 1) // Q == iota((width, width), 0) // Q)
    widen = as_ones(iota((TS, width), 1) // Q == iota((TS, width), 0))
    small = iota((TS, 1), 0)
    shuffle = as_ones(iota((TS, TS), 1) == (small % 8) * 4 + small // 8)
    across = ((1,), (1,))
    for top in range(span):
        at = slice(top * width, (top + 1) * width)
        x, y, z = (points_ref[k : k + 1, at] for k in range(3))
        weight = weights_ref[:, at]
        normal = normals_ref[:, top * TS : (top + 1) * TS]
        normal = jnp.concatenate([normal, jnp.zeros((1, TS), F32)], axis=0)
        face = left_rows(normal, jnp.zeros((1, TS), F32))
        face = lax.dot_general(shuffle, face, (across, ((), ())), preferred_element_type=F32)
        face_ref[top * TS : (top + 1) * TS] = face.astype(BF)
        wide = exact_dot(split(normal), widen)
        depth = wide[0:1] * x + wide[1:2] * y + wide[2:3] * z
        area = exact_dot(split(jnp.broadcast_to(weight, (8, width))), same)[0:1]
        scale = area / weight
        square = x * x + y * y + z * z + softening
        gap = jnp.concatenate([-2.0 * x * scale, -2.0 * y * scale, -2.0 * z * scale, scale], axis=0)
        gap = left_rows(gap, square * scale)
        gap = lax.dot_general(order, gap, (across, ((), ())), preferred_element_type=F32)
        gap_ref[top * Q : (top + 1) * Q] = gap.astype(BF).reshape(Q, TS, 32)
        parts = [jnp.broadcast_to(part, (128, width)).astype(BF) for part in split(depth)]
        deep = [lax.dot_general(order, part, (across, ((), ())), preferred_element_type=F32) for part in parts]
        depth_ref[top * Q : (top + 1) * Q] = (deep[0] + deep[1] + deep[2]).reshape(Q, TS, 128)
    list_work(visible_ref, mask_ref, across_ref, down_ref, capacity, total_ref, groups_ref, units_ref, slot_ref)
    gap_ref[span * Q] = jnp.where(iota((TS, 32), 1) == 24, 1.0, 0.0).astype(BF)
    depth_ref[span * Q] = jnp.zeros((TS, 128), F32)


def prepare(points, weights, normals, visible, quad_mask, owners, capacity):
    vmem = pl.BlockSpec(memory_space=pltpu.VMEM)
    pairs = normals.shape[1] // TS * Q
    tiles = owners.shape[0]
    whole = lambda *shape: jax.ShapeDtypeStruct(shape, jnp.int32)
    return pl.pallas_call(
        functools.partial(prepare_kernel, capacity),
        in_specs=[vmem] * 7,
        out_specs=[vmem] * 7,
        out_shape=[
            whole(1, 1),
            whole(1, 128),
            whole(pairs, 128),
            whole(1, tiles),
            jax.ShapeDtypeStruct((pairs + 1, TS, 32), BF),
            jax.ShapeDtypeStruct((pairs + 1, TS, 128), F32),
            jax.ShapeDtypeStruct((normals.shape[1], 32), BF),
        ],
        compiler_params=pltpu.CompilerParams(vmem_limit_bytes=40 * 2**20),
    )(points, weights, normals, visible, quad_mask, owners.reshape(1, tiles), owners.reshape(tiles, 1))


def column_features(packed_ref, rhs_ref, source):
    width = TS * Q
    span = rhs_ref.shape[0] // packed_ref.shape[0]
    ones = jnp.where(lax.broadcasted_iota(jnp.int32, (8, 128), 0) < 3, 1.0, 0.0)
    for tile in range(span):
        base = span * Q + tile * 3
        nx, ny, nz = (packed_ref[source, base + k : base + k + 1] for k in range(3))
        for lanes in range(width // 128):
            at = tile * Q + lanes * 4
            x, y, z, w = (packed_ref[source, at + k : at + k + 1] for k in range(4))
            square = x * x + y * y + z * z
            depth = nx * x + ny * y + nz * z
            scale = w * (1.0 / math.pi)
            half = scale * -0.5
            four = [x, y, z, square]
            rhs_ref[source * span + tile, :, lanes * 128 : (lanes + 1) * 128] = right_rows(by_rows((8, 128), four + four), ones)
            four = [nx * half, ny * half, nz * half, -depth * scale]
            start = width + lanes * 128
            rhs_ref[source * span + tile, :, start : start + 128] = right_rows(by_rows((8, 128), four + four), ones * 0.0)


def tiles_kernel(
    total_ref, groups_ref, units_ref, slot_ref, lhs_hbm, depth_hbm, face_hbm, packed_ref, out_ref,
    acc, near, rhs_ref, lhs_ref, depth_ref, face_ref, arrived,
):
    far = (face_hbm, lhs_hbm, depth_hbm)
    copies = [
        pltpu.make_async_copy(source, target, arrived.at[k])
        for k, (source, target) in enumerate(zip(far, (face_ref, lhs_ref, depth_ref)))
    ]
    for copy in copies:
        copy.start()
    out_ref[...] = jnp.zeros_like(out_ref)
    acc[...] = jnp.zeros_like(acc)
    width = TS * Q
    last = rhs_ref.shape[0] - 1

    def codes_of(place):
        tile, at = place
        return [units_ref[at * GROUP + g, tile] for g in range(GROUP)]

    def following(place):
        tile, at = place
        done = at + 1 >= groups_ref[0, tile]
        return (jnp.where(done, tile + 1, tile), jnp.where(done, 0, at + 1))

    def work_on(place):
        codes = codes_of(place)
        rows = [code % 128 for code in codes]
        tile = jnp.minimum(place[0], last)
        gap = jnp.concatenate([lhs_ref[r] for r in rows], axis=0)
        tops = [pl.ds(pl.multiple_of(jnp.minimum(r // Q, 3) * TS, TS), TS) for r in rows]
        total = [None] * GROUP
        for part in range(width // 256):
            at = slice(part * 256, (part + 1) * 256)
            ours = rhs_ref[tile, :, at]
            theirs = rhs_ref[tile, :, width + part * 256 : width + (part + 1) * 256]
            spread = jnp.dot(gap, ours, preferred_element_type=F32)
            cos_col = jnp.dot(gap, theirs, preferred_element_type=F32)
            value = jnp.maximum(cos_col, 0.0) * pl.reciprocal(spread * spread, approx=True)
            for g in range(GROUP):
                depth = depth_ref[rows[g]]
                for half in range(2):
                    lanes = slice(part * 256 + half * 128, part * 256 + (half + 1) * 128)
                    piece = jnp.maximum(near[tile, tops[g], lanes] - depth, 0.0) * value[g * TS : (g + 1) * TS, half * 128 : (half + 1) * 128]
                    total[g] = piece if total[g] is None else total[g] + piece
        return codes, total

    def some_groups(count):
        def run(_, place):
            for _ in range(count):
                codes, total = work_on(place)
                place = following(place)
                for g in range(GROUP):
                    tile = codes[g] // 128
                    acc[tile] = acc[tile] + total[g]
            return place

        return run

    def gather(source, _):
        column_features(packed_ref, rhs_ref, source)
        return 0

    lax.fori_loop(0, packed_ref.shape[0], gather, 0)

    def faces(step, _):
        for k in range(8):
            near[step * 8 + k] = jnp.dot(face_ref[...], rhs_ref[step * 8 + k, :, :width], preferred_element_type=F32)
        return 0

    copies[0].wait()
    lax.fori_loop(0, rhs_ref.shape[0] // 8, faces, 0)
    copies[1].wait()
    copies[2].wait()
    whole = total_ref[0, 0] // DEEP
    rest = total_ref[0, 0] - whole * DEEP
    place = lax.fori_loop(0, whole, some_groups(DEEP), (jnp.int32(0), jnp.int32(0)))
    lax.fori_loop(0, (rest + REST - 1) // REST, some_groups(REST), place)

    lane = lax.broadcasted_iota(jnp.int32, (8, 128), 1)
    second = (lane // TS) % 2 == 1
    upper = lane // (2 * TS) == 1

    def fold(step, _):
        for k in range(FOLD):
            tile = step * FOLD + k
            a0, a1, a2, a3 = [acc[tile, v * 8 : v * 8 + 8] for v in range(4)]
            low = jnp.where(second, a1, a0) + pltpu.roll(jnp.where(second, a0, a1), TS, 1)
            high = jnp.where(second, a3, a2) + pltpu.roll(jnp.where(second, a2, a3), TS, 1)
            mixed = jnp.where(upper, high, low) + pltpu.roll(jnp.where(upper, low, high), 2 * TS, 1)
            out_ref[slot_ref[0, tile]] = mixed
        return 0

    lax.fori_loop(0, acc.shape[0] // FOLD, fold, 0)


def assemble(total, groups, units, slot, lhs, depth, face, packed, slots):
    smem = pl.BlockSpec(memory_space=pltpu.SMEM)
    vmem = pl.BlockSpec(memory_space=pltpu.VMEM)
    tiles = slot.shape[1]
    columns = tiles * TS // face.shape[0]
    return pl.pallas_call(
        tiles_kernel,
        in_specs=[smem] * 4 + [pl.BlockSpec(memory_space=pl.ANY)] * 3 + [vmem],
        out_specs=vmem,
        out_shape=jax.ShapeDtypeStruct((slots, 8, 128), F32),
        scratch_shapes=[
            pltpu.VMEM((tiles, TS, 128), F32),
            pltpu.VMEM((columns, face.shape[0], TS * Q), F32),
            pltpu.VMEM((columns, 32, 2 * TS * Q), BF),
            pltpu.VMEM(lhs.shape, BF),
            pltpu.VMEM(depth.shape, F32),
            pltpu.VMEM(face.shape, BF),
            pltpu.SemaphoreType.DMA((3,)),
        ],
        compiler_params=pltpu.CompilerParams(vmem_limit_bytes=34 * 2**20),
    )(total, groups, units, slot, lhs, depth, face, packed)


def pack_kernel(points_ref, weights_ref, normals_ref, out_ref, held):
    width = TS * Q
    span = normals_ref.shape[1] // TS
    lane = lax.broadcasted_iota(jnp.int32, (1, width), 1)
    wanted = (lane % TS) * Q + lane // TS
    order = jnp.where(lax.broadcasted_iota(jnp.int32, (width, width), 0) == wanted, 1.0, 0.0).astype(BF)
    rows = []
    for tile in range(span):
        at = slice(tile * width, (tile + 1) * width)
        rows += [points_ref[:, at], weights_ref[:, at]]
    rows = exact_dot(split(jnp.concatenate(rows, axis=0)), order)
    held[...] = jnp.zeros_like(held)
    for tile in range(span):
        for lanes in range(width // 128):
            at = tile * Q + lanes * 4
            held[at : at + 4] = rows[tile * 4 : tile * 4 + 4, lanes * 128 : (lanes + 1) * 128]
        normal = normals_ref[:, tile * TS : (tile + 1) * TS]
        at = span * Q + tile * 3
        held[at : at + 3] = jnp.concatenate([normal] * 4, axis=1)
    for receiver in range(out_ref.shape[0]):
        out_ref[receiver] = held[...]


def pack_columns(points, weights, normals, receivers):
    vmem = pl.BlockSpec(memory_space=pltpu.VMEM)
    rows = normals.shape[1] // TS * (Q + 3)
    rows += -rows % 8
    return pl.pallas_call(
        pack_kernel,
        in_specs=[vmem] * 3,
        out_specs=vmem,
        out_shape=jax.ShapeDtypeStruct((receivers, rows, 128), F32),
        scratch_shapes=[pltpu.VMEM((rows, 128), F32)],
        compiler_params=pltpu.CompilerParams(vmem_limit_bytes=60 * 2**20),
    )(points, weights, normals)


def on_device(points, normals, weights, visible, quad_mask, owners):
    devices = lax.axis_size("rows") * lax.axis_size("blk")
    sources = lax.axis_size("blk")
    capacity = max(2, 2 * owners.shape[1] // devices)
    weights = weights[None]
    spread = pack_columns(points, weights, normals, sources)
    gathered = lax.all_to_all(spread, "blk", split_axis=0, concat_axis=0, tiled=True)
    ready = prepare(points, weights, normals, visible, quad_mask, owners[0, :, 0], capacity)
    out = assemble(*ready, gathered, devices * capacity)
    arrived = lax.all_to_all(
        out.reshape(devices, capacity * 8, 128), ("rows", "blk"), split_axis=0, concat_axis=0, tiled=True
    )
    return arrived.reshape(devices * capacity, TS * TS)


def solution(mesh):
    placed = (
        P(None, ("rows", "blk")),
        P(None, ("rows", "blk")),
        P(("rows", "blk")),
        P(("rows", "blk"), None),
        P(("rows", "blk"), None),
        P(("rows", "blk"), None, None),
    )
    return jax.shard_map(
        on_device, mesh=mesh, in_specs=placed, out_specs=P(("rows", "blk"), None), check_vma=False
    )
```
